32 devices in a mesh: groups: 2 (over y), dp: 4 (over z), tensor: 2 (over x), store: 2 (over core).
Axes of the slice: x: 2, y: 2, z: 4, core: 2. Of those that a mesh axis runs over, the one named last changes fastest.
Arguments:
- layer_inputs: bfloat16 [8, 32, 128, 4096], P(None, ('groups', 'dp', 'store'), None, 'tensor'), parts along dimension 1, may hold values from -6 to 6
- kv_grads: bfloat16 [8, 2, 32, 128, 1024], P(None, None, ('groups', 'dp', 'store'), None, 'tensor'), parts along dimension 2, may hold values from -6 to 6
- in_proj: bfloat16 [8, 64, 4096], P(None, None, 'tensor'), may hold values from -0.0078125 to 0.0078125
- out_proj: bfloat16 [8, 2, 64, 1024], P(None, None, None, 'tensor'), may hold values from -0.1875 to 0.1875
- owner_map: int32 [16], replicated, may hold values from 0 to 15, each once
Outputs:
- stored_rows: float32 [16, 32, 4096], P('dp', 'groups', ('tensor', 'store')), parts along dimension 1
The draws below stay inside these ranges and needn't reach their ends.
There are 2 independent parts, one for each index of `groups`. The reference program is written for one: setup_inputs(seed, part) draws one part's arguments, and reference() takes and returns one part's arrays. A program takes and returns all parts, laid end to end along the dimension named above; an argument that names none is the same for every part. Nothing has to cross between parts.
Inputs may be any that keep to these rules, and one draw needn't show every extreme that they name: owner_map names every layer block once.
All inputs are finite; a program needn't handle non-finite values.
Results may differ from the reference program's by a relative error of at most 0.0003.
Values sent between devices are 32-bit elements; how exact they have to be, the bound alone decides.
A program may use at most 64 MiB of HBM per device.

```python
import jax
import jax.numpy as jnp
from jax import lax

D = 4096
KV = 1024
RANK = 64
LAYERS = 8
SEQ = 128
EXAMPLES = 16
BLOCKS = 16


def levels(rng, extent, cuts, smallest, high):
    loudness, own = 1.0, jax.random.fold_in(rng, 6)
    for axis_at, shards_of in cuts:
        heights = jnp.exp(jax.random.uniform(jax.random.fold_in(own, axis_at), (shards_of,), jnp.float32, smallest / len(cuts), high / len(cuts)))
        loudness = loudness * jnp.repeat(heights, extent[axis_at] // shards_of).reshape([-1 if axis == axis_at else 1 for axis in range(len(extent))])
    return loudness


def gaussian(rng, shape, deviation, most, split=(), kind=jnp.bfloat16):
    result = deviation * jax.random.normal(rng, shape, jnp.float32)
    if split:
        result = result * levels(rng, shape, split, -0.22, 0.18)
    return jnp.clip(result, -most, most).astype(kind)


def setup_inputs(seed: int = 0, part: int = 0) -> dict:
    keys = jax.random.split(jax.random.key(seed), 6)
    own_keys = jax.random.split(jax.random.fold_in(keys[5], part), 6)
    return {
        "layer_inputs": gaussian(own_keys[0], (LAYERS, EXAMPLES, SEQ, D), 1.0, 6.0, ((1, 8), (3, 2))),
        "kv_grads": gaussian(own_keys[1], (LAYERS, 2, EXAMPLES, SEQ, KV), 1.0, 6.0, ((2, 8), (4, 2))),
        "in_proj": gaussian(keys[2], (LAYERS, RANK, D), (D * SEQ) ** -0.5, 0.0078125, ((2, 2),)),
        "out_proj": gaussian(keys[3], (LAYERS, 2, RANK, KV), KV ** -0.5, 0.1875, ((3, 2),)),
        "owner_map": jax.random.permutation(keys[4], BLOCKS).astype(jnp.int32),
    }


def reference(layer_inputs, kv_grads, in_proj, out_proj, owner_map):
    collected = []
    for layer_index in range(LAYERS):
        rows = layer_inputs[layer_index].reshape(EXAMPLES * SEQ, D)
        input_side = jnp.dot(rows, in_proj[layer_index].T, preferred_element_type=jnp.float32).reshape(EXAMPLES, SEQ, RANK)
        for projection in range(2):
            grad_rows = kv_grads[layer_index, projection].reshape(EXAMPLES * SEQ, KV)
            output_side = jnp.dot(grad_rows, out_proj[layer_index, projection].T, preferred_element_type=jnp.float32).reshape(EXAMPLES, SEQ, RANK)
            outer = jnp.einsum("esr,esc->erc", output_side, input_side, precision=lax.Precision.HIGHEST)
            collected.append(outer.reshape(EXAMPLES, RANK * RANK))
    gradients = jnp.stack(collected)
    return jnp.take(gradients, owner_map, axis=0)
```

```python
import functools

import jax
import jax.numpy as jnp
from jax import lax
from jax.experimental import pallas as pl
from jax.experimental.pallas import tpu as pltpu
from jax.sharding import PartitionSpec as P

MESH = pl.DeviceIdType.MESH
AHEAD = 3
LAG = 3


def dot_nt(a, b):
    return lax.dot_general(a, b, (((1,), (1,)), ((), ())), preferred_element_type=jnp.float32)


def split(x):
    high = x.astype(jnp.bfloat16)
    low = (x - high.astype(jnp.float32)).astype(jnp.bfloat16)
    return high, low


def kernel(
    dp, tn, st, owner_ref, x_hbm, kv_hbm, win_hbm, wout_hbm, out_ref,
    x, kv, win, wout, in_part, in_recv, in_terms, out_terms, g_part, g_recv, g_sum,
    load_sem, in_send_sem, in_recv_sem, g_send_sem, g_recv_sem, z_send_sem, z_recv_sem,
):
    layers, examples, seq, features = x.shape
    rank, key_part = wout.shape[2], wout.shape[3]
    blocks = 2 * layers
    per_owner = blocks // dp
    pairs = rank // 2
    quarter = pairs // (tn * st)
    my_z, my_t, my_s = lax.axis_index("dp"), lax.axis_index("tensor"), lax.axis_index("store")
    me = my_z * st + my_s

    def loads(l):
        return (
            pltpu.make_async_copy(win_hbm.at[l], win.at[l], load_sem.at[l, 0]),
            pltpu.make_async_copy(x_hbm.at[l], x.at[l], load_sem.at[l, 1]),
        )

    def out_loads(l):
        return (
            pltpu.make_async_copy(wout_hbm.at[l], wout.at[l], load_sem.at[l, 2]),
            pltpu.make_async_copy(kv_hbm.at[l], kv.at[l], load_sem.at[l, 3]),
        )

    def start(copies):
        for copy in copies:
            copy.start()

    def wait(copies):
        for copy in copies:
            copy.wait()

    for l in range(AHEAD):
        start(loads(l))

    barrier = pltpu.get_barrier_semaphore()
    for d in range(1, tn):
        pl.semaphore_signal(
            barrier, inc=1, device_id={"tensor": lax.rem(my_t + d, tn)}, device_id_type=MESH
        )
    for d in range(1, dp * st):
        other = lax.rem(me + d, dp * st)
        pl.semaphore_signal(
            barrier, inc=1, device_id={"dp": other // st, "store": lax.rem(other, st)}, device_id_type=MESH
        )

    def in_copy(l, d):
        return pltpu.make_async_remote_copy(
            src_ref=in_part.at[l], dst_ref=in_recv.at[l, d - 1],
            send_sem=in_send_sem.at[l, d - 1], recv_sem=in_recv_sem.at[l, d - 1],
            device_id={"tensor": lax.rem(my_t + d, tn)}, device_id_type=MESH,
        )

    for l in range(layers):
        wait(loads(l))
        if l + AHEAD < layers:
            start(loads(l + AHEAD))
        else:
            start(out_loads(l + AHEAD - layers))
        in_part[l] = dot_nt(win[l], x[l].reshape(examples * seq, features))
        if l == 0:
            pl.semaphore_wait(barrier, tn - 1 + dp * st - 1)
        for d in range(1, tn):
            in_copy(l, d).start()

    row = lax.broadcasted_iota(jnp.int32, (rank, rank), 0)
    col = lax.broadcasted_iota(jnp.int32, (rank, rank), 1)
    source = jnp.where(row < pairs, 2 * row, 2 * (row - pairs) + 1)
    reorder = jnp.where(col == source, 1.0, 0.0).astype(jnp.bfloat16)

    for l in range(layers):
        wait(out_loads(l))
        if l + AHEAD < layers:
            start(out_loads(l + AHEAD))
        for p in range(2):
            weight = jnp.dot(reorder, wout[l, p], preferred_element_type=jnp.float32)
            side = dot_nt(weight.astype(jnp.bfloat16), kv[l, p].reshape(examples * seq, key_part))
            high, low = split(side)
            for e in range(examples):
                own = slice(e * seq, (e + 1) * seq)
                out_terms[2 * l + p, e, :, 0:seq] = high[:, own]
                out_terms[2 * l + p, e, :, seq:2 * seq] = high[:, own]
                out_terms[2 * l + p, e, :, 2 * seq:3 * seq] = low[:, own]

    for l in range(layers):
        side = in_part[l]
        for d in range(1, tn):
            in_copy(l, d).wait_recv()
            side = side + in_recv[l, d - 1]
        high, low = split(side)
        for e in range(examples):
            own = slice(e * seq, (e + 1) * seq)
            in_terms[l, e, :, 0:seq] = high[:, own]
            in_terms[l, e, :, seq:2 * seq] = low[:, own]
            in_terms[l, e, :, 2 * seq:3 * seq] = high[:, own]

    def place(n):
        z = lax.rem(my_z + 1 + n % dp, dp)
        k = n // dp
        return z, k, z * per_owner + k

    def g_copy(j, d):
        return pltpu.make_async_remote_copy(
            src_ref=g_part.at[j, lax.rem(my_t + d, tn)], dst_ref=g_recv.at[j, d - 1],
            send_sem=g_send_sem.at[j, d - 1], recv_sem=g_recv_sem.at[j, d - 1],
            device_id={"tensor": lax.rem(my_t + d, tn)}, device_id_type=MESH,
        )

    def z_copy(n, s):
        z, k, j = place(n)
        to = lax.rem(my_s + s, st)
        return pltpu.make_async_remote_copy(
            src_ref=g_sum.at[j, to], dst_ref=out_ref.at[k, me],
            send_sem=z_send_sem.at[j, s], recv_sem=z_recv_sem.at[k, me],
            device_id={"dp": z, "store": to}, device_id_type=MESH,
        )

    def stays(n, s):
        return s == 0 and (n + 1) % dp == 0

    def partial(n):
        _, _, j = place(n)
        block = owner_ref[j]
        for e in range(examples):
            g = dot_nt(out_terms[block, e], in_terms[block // 2, e])
            g = jnp.concatenate([g[:pairs], g[pairs:]], axis=1)
            for c in range(tn * st):
                g_part[j, c // st, c % st, e] = g[c * quarter:(c + 1) * quarter]
        for d in range(1, tn):
            g_copy(j, d).start()

    def total(n):
        _, k, j = place(n)
        whole = g_part[j, my_t]
        for d in range(1, tn):
            g_copy(j, d).wait_recv()
            whole = whole + g_recv[j, d - 1]
        g_sum[j] = whole
        for s in range(st):
            if stays(n, s):
                out_ref[k, me] = g_sum[j, my_s]
            else:
                z_copy(n, s).start()

    for n in range(blocks + LAG):
        if n < blocks:
            partial(n)
        if n >= LAG:
            total(n - LAG)

    for l in range(layers):
        for d in range(1, tn):
            in_copy(l, d).wait_send()
    for n in range(blocks):
        for d in range(1, tn):
            g_copy(place(n)[2], d).wait_send()
        for s in range(st):
            if not stays(n, s):
                z_copy(n, s).wait_send()
    for k in range(per_owner):
        for d in range(1, dp * st):
            other = lax.rem(me + d, dp * st)
            pltpu.make_async_remote_copy(
                src_ref=out_ref.at[k, other], dst_ref=out_ref.at[k, other],
                send_sem=z_send_sem.at[0, 0], recv_sem=z_recv_sem.at[k, other],
                device_id={"dp": other // st, "store": lax.rem(other, st)}, device_id_type=MESH,
            ).wait_recv()


def shards(dp, tn, st, layer_inputs, kv_grads, in_proj, out_proj, owner_map):
    layers, examples, seq, features = layer_inputs.shape
    rank = in_proj.shape[1]
    blocks = 2 * layers
    per_owner = blocks // dp
    quarter = rank // 2 // (tn * st)
    lanes = 2 * rank
    hbm = pl.BlockSpec(memory_space=pltpu.HBM)
    dma = pltpu.SemaphoreType.DMA
    others = max(tn - 1, 1)
    stored = pl.pallas_call(
        functools.partial(kernel, dp, tn, st),
        out_shape=jax.ShapeDtypeStruct((per_owner, dp * st, examples, quarter, lanes), jnp.float32),
        in_specs=[pl.BlockSpec(memory_space=pltpu.SMEM), hbm, hbm, hbm, hbm],
        out_specs=pl.BlockSpec(memory_space=pltpu.VMEM),
        scratch_shapes=[
            pltpu.VMEM(layer_inputs.shape, jnp.bfloat16),
            pltpu.VMEM(kv_grads.shape, jnp.bfloat16),
            pltpu.VMEM(in_proj.shape, jnp.bfloat16),
            pltpu.VMEM(out_proj.shape, jnp.bfloat16),
            pltpu.VMEM((layers, rank, examples * seq), jnp.float32),
            pltpu.VMEM((layers, others, rank, examples * seq), jnp.float32),
            pltpu.VMEM((layers, examples, rank, 3 * seq), jnp.bfloat16),
            pltpu.VMEM((blocks, examples, rank, 3 * seq), jnp.bfloat16),
            pltpu.VMEM((blocks, tn, st, examples, quarter, lanes), jnp.float32),
            pltpu.VMEM((blocks, others, st, examples, quarter, lanes), jnp.float32),
            pltpu.VMEM((blocks, st, examples, quarter, lanes), jnp.float32),
            dma((layers, 4)),
            dma((layers, others)),
            dma((layers, others)),
            dma((blocks, others)),
            dma((blocks, others)),
            dma((blocks, st)),
            dma((per_owner, dp * st)),
        ],
        compiler_params=pltpu.CompilerParams(
            collective_id=0, has_side_effects=True, vmem_limit_bytes=56 * 1024 * 1024
        ),
    )(owner_map, layer_inputs, kv_grads, in_proj, out_proj)
    return stored.reshape(per_owner, dp * st * examples, quarter * lanes)


def solution(mesh):
    in_specs = (
        P(None, ("groups", "dp", "store"), None, "tensor"),
        P(None, None, ("groups", "dp", "store"), None, "tensor"),
        P(None, None, "tensor"),
        P(None, None, None, "tensor"),
        P(),
    )
    out_specs = P("dp", "groups", ("tensor", "store"))
    return jax.shard_map(
        functools.partial(shards, mesh.shape["dp"], mesh.shape["tensor"], mesh.shape["store"]),
        mesh=mesh, in_specs=in_specs, out_specs=out_specs, check_vma=False,
    )
```

```python
import functools

import jax
import jax.numpy as jnp
from jax import lax
from jax.experimental import pallas as pl
from jax.experimental.pallas import tpu as pltpu
from jax.sharding import PartitionSpec as P

MESH = pl.DeviceIdType.MESH
AHEAD = 3


def dot_nt(a, b):
    return lax.dot_general(a, b, (((1,), (1,)), ((), ())), preferred_element_type=jnp.float32)


def split(x):
    high = x.astype(jnp.bfloat16)
    low = (x - high.astype(jnp.float32)).astype(jnp.bfloat16)
    return high, low


def kernel(
    dp, tn, st, owner_ref, x_hbm, kv_hbm, win_hbm, wout_hbm, out_ref,
    x, kv, win, wout, in_part, in_recv, in_terms, out_terms, g_part, g_recv, g_sum,
    load_sem, in_send_sem, in_recv_sem, g_send_sem, g_recv_sem, z_send_sem, z_recv_sem,
):
    layers, examples, seq, features = x.shape
    rank, key_part = wout.shape[2], wout.shape[3]
    blocks = 2 * layers
    per_owner = blocks // dp
    pairs = rank // 2
    quarter = pairs // (tn * st)
    halves = 2 if dp % 2 == 0 else 1
    half = dp // halves
    my_z, my_t, my_s = lax.axis_index("dp"), lax.axis_index("tensor"), lax.axis_index("store")
    me = my_z * st + my_s

    def loads(l):
        return (
            pltpu.make_async_copy(win_hbm.at[l], win.at[l], load_sem.at[l, 0]),
            pltpu.make_async_copy(x_hbm.at[l], x.at[l], load_sem.at[l, 1]),
        )

    def out_loads(l):
        return (
            pltpu.make_async_copy(wout_hbm.at[l], wout.at[l], load_sem.at[l, 2]),
            pltpu.make_async_copy(kv_hbm.at[l], kv.at[l], load_sem.at[l, 3]),
        )

    def start(copies):
        for copy in copies:
            copy.start()

    def wait(copies):
        for copy in copies:
            copy.wait()

    for l in range(AHEAD):
        start(loads(l))

    barrier = pltpu.get_barrier_semaphore()
    for d in range(1, tn):
        pl.semaphore_signal(
            barrier, inc=1, device_id={"tensor": lax.rem(my_t + d, tn)}, device_id_type=MESH
        )
    for d in range(1, dp * st):
        other = lax.rem(me + d, dp * st)
        pl.semaphore_signal(
            barrier, inc=1, device_id={"dp": other // st, "store": lax.rem(other, st)}, device_id_type=MESH
        )

    def in_copy(l, d):
        return pltpu.make_async_remote_copy(
            src_ref=in_part.at[l], dst_ref=in_recv.at[l, d - 1],
            send_sem=in_send_sem.at[l, d - 1], recv_sem=in_recv_sem.at[l, d - 1],
            device_id={"tensor": lax.rem(my_t + d, tn)}, device_id_type=MESH,
        )

    for l in range(layers):
        wait(loads(l))
        if l + AHEAD < layers:
            start(loads(l + AHEAD))
        else:
            start(out_loads(l + AHEAD - layers))
        in_part[l] = dot_nt(win[l], x[l].reshape(examples * seq, features))
        if l == 0:
            pl.semaphore_wait(barrier, tn - 1 + dp * st - 1)
        for d in range(1, tn):
            in_copy(l, d).start()

    row = lax.broadcasted_iota(jnp.int32, (rank, rank), 0)
    col = lax.broadcasted_iota(jnp.int32, (rank, rank), 1)
    source = jnp.where(row < pairs, 2 * row, 2 * (row - pairs) + 1)
    reorder = jnp.where(col == source, 1.0, 0.0).astype(jnp.bfloat16)

    for l in range(layers):
        wait(out_loads(l))
        if l + AHEAD < layers:
            start(out_loads(l + AHEAD))
        for p in range(2):
            weight = jnp.dot(reorder, wout[l, p], preferred_element_type=jnp.float32)
            side = dot_nt(weight.astype(jnp.bfloat16), kv[l, p].reshape(examples * seq, key_part))
            high, low = split(side)
            for e in range(examples):
                own = slice(e * seq, (e + 1) * seq)
                out_terms[2 * l + p, e, :, 0:seq] = high[:, own]
                out_terms[2 * l + p, e, :, seq:2 * seq] = high[:, own]
                out_terms[2 * l + p, e, :, 2 * seq:3 * seq] = low[:, own]

    for l in range(layers):
        side = in_part[l]
        for d in range(1, tn):
            in_copy(l, d).wait_recv()
            side = side + in_recv[l, d - 1]
        high, low = split(side)
        for e in range(examples):
            own = slice(e * seq, (e + 1) * seq)
            in_terms[l, e, :, 0:seq] = high[:, own]
            in_terms[l, e, :, seq:2 * seq] = low[:, own]
            in_terms[l, e, :, 2 * seq:3 * seq] = high[:, own]

    def place(n):
        turn, k = n // per_owner, n % per_owner
        side = lax.rem(my_z // half + 1 + turn // half, halves)
        z = side * half + lax.rem(my_z + 1 + turn, half)
        return z, k, z * per_owner + k

    def g_copy(j, d):
        return pltpu.make_async_remote_copy(
            src_ref=g_part.at[j, lax.rem(my_t + d, tn)], dst_ref=g_recv.at[j, d - 1],
            send_sem=g_send_sem.at[j, d - 1], recv_sem=g_recv_sem.at[j, d - 1],
            device_id={"tensor": lax.rem(my_t + d, tn)}, device_id_type=MESH,
        )

    def z_copy(n, s):
        z, k, j = place(n)
        to = lax.rem(my_s + s, st)
        return pltpu.make_async_remote_copy(
            src_ref=g_sum.at[j, to], dst_ref=out_ref.at[k, me],
            send_sem=z_send_sem.at[j, s], recv_sem=z_recv_sem.at[k, me],
            device_id={"dp": z, "store": to}, device_id_type=MESH,
        )

    def stays(n, s):
        return s == 0 and n // per_owner == dp - 1

    def partial(n):
        _, _, j = place(n)
        block = owner_ref[j]
        for e in range(examples):
            g = dot_nt(out_terms[block, e], in_terms[block // 2, e])
            g = jnp.concatenate([g[:pairs], g[pairs:]], axis=1)
            for c in range(tn * st):
                g_part[j, c // st, c % st, e] = g[c * quarter:(c + 1) * quarter]
        for d in range(1, tn):
            g_copy(j, d).start()

    def total(n):
        _, k, j = place(n)
        whole = g_part[j, my_t]
        for d in range(1, tn):
            g_copy(j, d).wait_recv()
            whole = whole + g_recv[j, d - 1]
        g_sum[j] = whole
        for s in range(st):
            if stays(n, s):
                out_ref[k, me] = g_sum[j, my_s]
            else:
                z_copy(n, s).start()

    for n in range(blocks):
        partial(n)
    for n in range(blocks):
        total(n)

    for l in range(layers):
        for d in range(1, tn):
            in_copy(l, d).wait_send()
    for n in range(blocks):
        for d in range(1, tn):
            g_copy(place(n)[2], d).wait_send()
        for s in range(st):
            if not stays(n, s):
                z_copy(n, s).wait_send()
    for k in range(per_owner):
        for d in range(1, dp * st):
            other = lax.rem(me + d, dp * st)
            pltpu.make_async_remote_copy(
                src_ref=out_ref.at[k, other], dst_ref=out_ref.at[k, other],
                send_sem=z_send_sem.at[0, 0], recv_sem=z_recv_sem.at[k, other],
                device_id={"dp": other // st, "store": lax.rem(other, st)}, device_id_type=MESH,
            ).wait_recv()


def shards(dp, tn, st, layer_inputs, kv_grads, in_proj, out_proj, owner_map):
    layers, examples, seq, features = layer_inputs.shape
    rank = in_proj.shape[1]
    blocks = 2 * layers
    per_owner = blocks // dp
    quarter = rank // 2 // (tn * st)
    lanes = 2 * rank
    hbm = pl.BlockSpec(memory_space=pltpu.HBM)
    dma = pltpu.SemaphoreType.DMA
    others = max(tn - 1, 1)
    stored = pl.pallas_call(
        functools.partial(kernel, dp, tn, st),
        out_shape=jax.ShapeDtypeStruct((per_owner, dp * st, examples, quarter, lanes), jnp.float32),
        in_specs=[pl.BlockSpec(memory_space=pltpu.SMEM), hbm, hbm, hbm, hbm],
        out_specs=pl.BlockSpec(memory_space=pltpu.VMEM),
        scratch_shapes=[
            pltpu.VMEM(layer_inputs.shape, jnp.bfloat16),
            pltpu.VMEM(kv_grads.shape, jnp.bfloat16),
            pltpu.VMEM(in_proj.shape, jnp.bfloat16),
            pltpu.VMEM(out_proj.shape, jnp.bfloat16),
            pltpu.VMEM((layers, rank, examples * seq), jnp.float32),
            pltpu.VMEM((layers, others, rank, examples * seq), jnp.float32),
            pltpu.VMEM((layers, examples, rank, 3 * seq), jnp.bfloat16),
            pltpu.VMEM((blocks, examples, rank, 3 * seq), jnp.bfloat16),
            pltpu.VMEM((blocks, tn, st, examples, quarter, lanes), jnp.float32),
            pltpu.VMEM((blocks, others, st, examples, quarter, lanes), jnp.float32),
            pltpu.VMEM((blocks, st, examples, quarter, lanes), jnp.float32),
            dma((layers, 4)),
            dma((layers, others)),
            dma((layers, others)),
            dma((blocks, others)),
            dma((blocks, others)),
            dma((blocks, st)),
            dma((per_owner, dp * st)),
        ],
        compiler_params=pltpu.CompilerParams(
            collective_id=0, has_side_effects=True, vmem_limit_bytes=56 * 1024 * 1024
        ),
    )(owner_map, layer_inputs, kv_grads, in_proj, out_proj)
    return stored.reshape(per_owner, dp * st * examples, quarter * lanes)


def solution(mesh):
    in_specs = (
        P(None, ("groups", "dp", "store"), None, "tensor"),
        P(None, None, ("groups", "dp", "store"), None, "tensor"),
        P(None, None, "tensor"),
        P(None, None, None, "tensor"),
        P(),
    )
    out_specs = P("dp", "groups", ("tensor", "store"))
    return jax.shard_map(
        functools.partial(shards, mesh.shape["dp"], mesh.shape["tensor"], mesh.shape["store"]),
        mesh=mesh, in_specs=in_specs, out_specs=out_specs, check_vma=False,
    )
```
